1024 devices in a mesh: node: 16 (over z), local: 64 (over x, y, core).
Axes of the slice: x: 4, y: 8, z: 16, core: 2. Of those that a mesh axis runs over, the one named last changes fastest.
Arguments:
- queries: bfloat16 [1024, 128, 576], P(('node', 'local')), may hold values from -64 to 64
- latent_cache: bfloat16 [1024, 320, 576], P(('node', 'local')), may hold values from -8 to 8
- lengths: int32 [1024], P(('node', 'local')), may hold values from 2 to 320, as said below
- moe_rows: bfloat16 [1024, 7168], P(('node', 'local')), may hold values from -6 to 6
- expert_ids: int32 [1024, 8], P(('node', 'local')), may hold values from 0 to 63, as said below
- route_gates: bfloat16 [1024, 8], P(('node', 'local')), may hold values from 0.099609375 to 1
- w_gate: bfloat16 [1024, 64, 7168], P(('node', 'local')), may hold values from -0.0625 to 0.0625
- w_up: bfloat16 [1024, 64, 7168], P(('node', 'local')), may hold values from -0.0625 to 0.0625
- w_down: bfloat16 [1024, 64, 7168], P(('node', 'local')), may hold values from -0.1875 to 0.1875
Outputs:
- context: bfloat16 [1024, 128, 512], P(('node', 'local'))
- moe_out: bfloat16 [1024, 7168], P(('node', 'local'))
The draws below stay inside these ranges and needn't reach their ends.
Inputs may be any that keep to these rules, and one draw needn't show every extreme that they name: `expert_ids`: each token names 8 distinct experts in 4 groups, 2 in each; expert i is in group i // 4. For every l, among the 16 tokens whose index is l modulo 64, exactly 4 use each group, and each expert of that group is used by exactly 2 of them. `lengths`: some request has all 320 positions valid.
All inputs are finite; a program needn't handle non-finite values.
Results may differ from the reference program's by a relative error of at most 0.017.
Values may be sent and summed in bfloat16 or wider, within the bound.
A program may use at most 32 MiB of HBM per device.

```python
import math
import jax
import jax.numpy as jnp
from jax import lax

D = 7168
HID = 1024
HEADS = 128
LATENT = 512
ROPE = 64
E_NODE = 4
TOPK = 8
GROUPS_PICKED = 4
CTX = 320
PER_GROUP = 2
REQUESTS = 1024
TOKENS = 1024
EXPERTS = 64
SLICES = 16
HID_DEV = 64
EXPERT_ROWS = 128
N_NODE = 16
N_LOCAL = 64


def shared_cache(key):
    return jnp.clip(jax.random.normal(key, (REQUESTS, CTX, LATENT + ROPE), jnp.float32), -6.0, 6.0)


def draw_latent_cache(key, part):
    base_rows = shared_cache(key)
    return base_rows.astype(jnp.bfloat16)


def draw_queries(key, part):
    key = jax.random.fold_in(key, 7)
    key_one = jax.random.fold_in(key, 0)
    drawn = jnp.clip(jax.random.normal(key_one, (REQUESTS, HEADS, LATENT + ROPE), jnp.float32), -6.0, 6.0)
    return drawn.astype(jnp.bfloat16)


def draw_lengths(key, part):
    key = jax.random.fold_in(key, 9)
    key_one, key_two = jax.random.split(key)
    length_draw = jax.random.randint(key_one, (REQUESTS,), 2, CTX + 1)
    forced_index = jax.random.randint(key_two, (), 0, REQUESTS)
    return length_draw.at[forced_index].set(CTX).astype(jnp.int32)


def one_class(class_key):
    key_one, key_two, key_three = jax.random.split(class_key, 3)
    sigma_perm = jax.random.permutation(key_one, N_NODE)
    tau_perm = jax.random.permutation(key_two, N_NODE)
    member = (jnp.mod(sigma_perm[None, :] - tau_perm[:, None], N_NODE) < GROUPS_PICKED).astype(jnp.int32)
    class_rank = jnp.cumsum(member, axis=0) - 1
    pick_place = jnp.cumsum(member, axis=1) - 1
    group_keys = jax.random.split(key_three, N_NODE)
    orders = jax.vmap(jax.random.permutation, in_axes=(0, None))(group_keys, E_NODE)
    entries = []
    for column in range(PER_GROUP):
        chosen_slot = jnp.mod(class_rank * PER_GROUP + column, E_NODE)
        local_expert = jnp.sum(orders[None, :, :] * (jnp.arange(E_NODE)[None, None, :] == chosen_slot[:, :, None]), axis=2)
        expert_number = jnp.arange(N_NODE)[None, :] * E_NODE + local_expert
        placed = member[:, :, None] * (pick_place[:, :, None] == jnp.arange(GROUPS_PICKED)[None, None, :])
        entries.append(jnp.sum(placed * expert_number[:, :, None], axis=1))
    return jnp.stack(entries, axis=2).reshape(N_NODE, TOPK)


def draw_expert_ids(key, part):
    key = jax.random.fold_in(key, 5)
    class_keys = jax.random.split(key, N_LOCAL)
    all_classes = jax.vmap(one_class)(class_keys)
    return jnp.transpose(all_classes, (1, 0, 2)).reshape(TOKENS, TOPK).astype(jnp.int32)


def levels(rng, shape, cuts, smallest, high):
    loudness, own = 1.0, jax.random.fold_in(rng, 6)
    for dim, parts in cuts:
        steps = jnp.exp(jax.random.uniform(jax.random.fold_in(own, dim), (parts,), jnp.float32, smallest / len(cuts), high / len(cuts)))
        loudness = loudness * jnp.repeat(steps, shape[dim] // parts).reshape([-1 if axis == dim else 1 for axis in range(len(shape))])
    return loudness


def noise(rng, extent, width, limit, cuts=(), kind=jnp.bfloat16):
    values = width * jax.random.normal(rng, extent, jnp.float32)
    if cuts:
        values = values * levels(rng, extent, cuts, -0.22, 0.18)
    return jnp.clip(values, -limit, limit).astype(kind)


def setup_inputs(seed: int = 0) -> dict:
    keys = jax.random.split(jax.random.key(seed), 10)
    queries = draw_queries(jax.random.fold_in(keys[9], 71), 0)
    latent_cache = draw_latent_cache(jax.random.fold_in(keys[9], 71), 0)
    lengths = draw_lengths(jax.random.fold_in(keys[9], 71), 0)
    moe_rows = noise(keys[3], (TOKENS, D), 1.0, 6.0, ((0, 1024),))
    expert_ids = draw_expert_ids(jax.random.fold_in(keys[9], 71), 0)
    route_gates = jnp.clip(jnp.exp(math.log(1.0) - 2.306499 * jax.random.uniform(keys[5], (TOKENS, TOPK), jnp.float32) ** levels(keys[5], (TOKENS, TOPK), ((0, 1024),), -0.2, 0.2)), 0.099609375, 1.0).astype(jnp.bfloat16)
    w_gate = noise(keys[6], (EXPERTS * SLICES, HID_DEV, D), D ** -0.5, 0.0625, ((0, 1024),))
    w_up = noise(keys[7], (EXPERTS * SLICES, HID_DEV, D), D ** -0.5, 0.0625, ((0, 1024),))
    w_down = noise(keys[8], (EXPERTS * SLICES, HID_DEV, D), HID ** -0.5, 0.1875, ((0, 1024),))
    return dict(queries=queries, latent_cache=latent_cache, lengths=lengths, moe_rows=moe_rows, expert_ids=expert_ids, route_gates=route_gates, w_gate=w_gate, w_up=w_up, w_down=w_down)


score_scale = 192.0 ** -0.5


def attend_request(inputs):
    query_heads, cache_rows, length = inputs
    scores = jnp.dot(query_heads, cache_rows.T, preferred_element_type=jnp.float32) * score_scale
    visible = (jnp.arange(CTX) < length)[None, :]
    scores = jnp.where(visible, scores, -1e30)
    highest = jnp.max(scores, axis=1, keepdims=True)
    weights = jnp.where(visible, jnp.exp(scores - highest), 0.0)
    probabilities = (weights / jnp.sum(weights, axis=1, keepdims=True)).astype(jnp.bfloat16)
    return jnp.dot(probabilities, cache_rows[:, :LATENT], preferred_element_type=jnp.float32).astype(jnp.bfloat16)


def reference(queries, latent_cache, lengths, moe_rows, expert_ids, route_gates, w_gate, w_up, w_down):
    context = lax.map(attend_request, (queries, latent_cache, lengths))
    flat_ids = expert_ids.reshape(-1)
    onehot = (flat_ids[:, None] == jnp.arange(EXPERTS)[None, :]).astype(jnp.int32)
    order_rank = jnp.sum((jnp.cumsum(onehot, axis=0) - onehot) * onehot, axis=1)
    row_of = jnp.arange(TOKENS * TOPK) // TOPK

    def run_expert(expert):
        pick_rows = jnp.nonzero(flat_ids == expert, size=EXPERT_ROWS)[0]
        token_rows = moe_rows[row_of[pick_rows]].astype(jnp.float32)
        start = (expert * SLICES).astype(jnp.int32)
        gate_slab = lax.dynamic_slice_in_dim(w_gate, start, SLICES, 0).astype(jnp.float32)
        up_slab = lax.dynamic_slice_in_dim(w_up, start, SLICES, 0).astype(jnp.float32)
        down_slab = lax.dynamic_slice_in_dim(w_down, start, SLICES, 0).astype(jnp.float32)
        gate_pre = jnp.einsum("rd,shd->srh", token_rows, gate_slab)
        up_pre = jnp.einsum("rd,shd->srh", token_rows, up_slab)
        hidden = (jax.nn.silu(gate_pre) * up_pre).astype(jnp.bfloat16)
        slice_out = jnp.einsum("srh,shd->srd", hidden.astype(jnp.float32), down_slab).astype(jnp.bfloat16)
        return jnp.sum(slice_out.astype(jnp.float32), axis=0)

    outputs = lax.map(run_expert, jnp.arange(EXPERTS, dtype=jnp.int32))
    picked_out = outputs[flat_ids, order_rank]
    weighted = (route_gates.reshape(-1).astype(jnp.float32)[:, None] * picked_out).reshape(TOKENS, TOPK, D)
    group_hot = ((expert_ids // E_NODE)[:, :, None] == jnp.arange(N_NODE)[None, None, :]).astype(jnp.float32)

    def combine_token(inputs):
        token_hot, token_terms = inputs
        node_part = jnp.dot(token_hot.T, token_terms, precision=lax.Precision.HIGHEST).astype(jnp.bfloat16)
        return jnp.sum(node_part.astype(jnp.float32), axis=0).astype(jnp.bfloat16)

    moe_out = lax.map(combine_token, (group_hot, weighted))
    return context, moe_out
```

```python
import jax
import jax.numpy as jnp
from jax import lax
from jax.experimental import pallas as pl
from jax.experimental.pallas import tpu as pltpu
from jax.sharding import PartitionSpec as P

MESH = pl.DeviceIdType.MESH
BF16, F32 = jnp.bfloat16, jnp.float32

D = 7168
HEADS = 128
CTX = 320
WIDTH = 576
LATENT = 512
HID = 64
EXPERTS = 64
E_NODE = 4
NZ, NX, NY, NC = 16, 4, 8, 2
PEERS = NX * NC
PIECE = 512
PIECES = D // PIECE
HALF = PIECES // 2
HALF_D = D // 2
ROWS = 16
GROUPS = ((0, 4), (4, 7))
SCALE = 192.0**-0.5


def iota(shape, dim):
    return lax.broadcasted_iota(jnp.int32, shape, dim)


def onehot(condition):
    return jnp.where(condition, 1.0, 0.0).astype(BF16)


def dot(a, b, dims=((1,), (0,))):
    return lax.dot_general(a, b, (dims, ((), ())), preferred_element_type=F32)


NT = ((1,), (1,))


def kernel(
    length_ref, block_ref, q_hbm, cache_hbm, gate_hbm, up_hbm, down_hbm,
    context_ref, out_ref,
    q_buf, cache_buf, score_buf, prob_buf, gu_buf, down_buf,
    z_buf, place_buf, x_send, x_recv, y_buf, pre_buf, pre_recv, part_buf,
    rs_send, rs_recv, b_send, b_recv, c_buf, c_recv, r_send, r_recv,
    in_sem, w_send_sem, w_recv_sem, z1_send, z1_recv, z2_send, z2_recv,
    x_ssem, x_rsem, y_ssem, y_rsem, p_ssem, p_rsem,
    s_ssem, s_rsem, b_ssem, b_rsem, c_ssem, c_rsem, r_ssem, r_rsem,
):
    g = lax.axis_index("node")
    l = lax.axis_index("local")
    x, y, c = l // 16, (l % 16) // 2, l % 2
    a, b = g // 4, g % 4
    me = x * NC + c
    other = 1 - c

    def at_z(step):
        return (lax.rem(g + step + NZ, NZ), l)

    def at_y(step):
        return (g, x * 16 + lax.rem(y + step + NY, NY) * 2 + c)

    def peer(n):
        return (g, (n // NC) * 16 + y * 2 + n % NC)

    twin = (g, l + 1 - 2 * c)

    def remote(src, dst, ssem, rsem, device):
        return pltpu.make_async_remote_copy(
            src_ref=src, dst_ref=dst, send_sem=ssem, recv_sem=rsem,
            device_id=device, device_id_type=MESH,
        )

    mine = pl.ds(pl.multiple_of(c * HALF_D, 128), HALF_D)
    theirs = pl.ds(pl.multiple_of(other * HALF_D, 128), HALF_D)
    own_copies = [
        pltpu.make_async_copy(q_hbm.at[0], q_buf, in_sem.at[0]),
        pltpu.make_async_copy(cache_hbm.at[0], cache_buf, in_sem.at[1]),
        pltpu.make_async_copy(gate_hbm.at[0, :, mine], gu_buf.at[c], in_sem.at[2]),
        pltpu.make_async_copy(up_hbm.at[0, :, mine], gu_buf.at[2 + c], in_sem.at[3]),
        pltpu.make_async_copy(down_hbm.at[0, :, mine], down_buf.at[c], in_sem.at[4]),
    ]
    for copy in own_copies:
        copy.start()
    sends = []

    barrier = pltpu.get_barrier_semaphore()
    z_steps = (1, -1, 2, -2, 4, 8, 12)
    partners = [at_z(s) for s in z_steps]
    partners += [peer(lax.rem(me + o, PEERS)) for o in range(1, PEERS)]
    partners += [at_y(1), at_y(-1)]
    for device in partners:
        pl.semaphore_signal(barrier, inc=1, device_id=device, device_id_type=MESH)
    z_buf[b, a] = block_ref[...]
    pl.semaphore_wait(barrier, len(partners))

    for o in range(1, 4):
        copy = remote(z_buf.at[b, a], z_buf.at[b, a], z1_send.at[o - 1], z1_recv.at[o - 1], at_z(4 * o))
        copy.start()
        sends.append(copy)
    for k, (hbm, buf, slot) in enumerate(
        ((gate_hbm, gu_buf, c), (up_hbm, gu_buf, 2 + c), (down_hbm, down_buf, c))
    ):
        copy = remote(hbm.at[0, :, theirs], buf.at[slot], w_send_sem.at[k], w_recv_sem.at[k], twin)
        copy.start()
        sends.append(copy)

    own_copies[0].wait()
    own_copies[1].wait()
    score_buf[...] = dot(q_buf[...], cache_buf[...], NT) * SCALE

    for o in range(1, 4):
        slot = z_buf.at[b, lax.rem(a - o + 4, 4)]
        remote(slot, slot, z1_send.at[o - 1], z1_recv.at[o - 1], at_z(4 * o)).wait_recv()
    far = 4 * (g % 2) - 2
    for k, step in enumerate((1, -1, far)):
        copy = remote(z_buf.at[b], z_buf.at[b], z2_send.at[k], z2_recv.at[k], at_z(step))
        copy.start()
        sends.append(copy)

    visible = iota((HEADS, CTX), 1) < length_ref[0]
    scores = jnp.where(visible, score_buf[...], -1e30)
    highest = jnp.max(scores, axis=1, keepdims=True)
    weights = jnp.where(visible, jnp.exp(scores - highest), 0.0)
    prob_buf[...] = (weights / jnp.sum(weights, axis=1, keepdims=True)).astype(BF16)

    col_x = iota((128, 256), 0) // 32
    col_h = iota((128, 256), 0) // 16 % 2
    col_k = iota((128, 256), 0) // 8 % 2
    col_j = iota((128, 256), 0) % 8
    row_j = iota((128, 256), 1) % 16
    expert_pick = onehot(iota((128, 128), 1) == E_NODE * g + iota((128, 128), 0) // 32)
    from_slot = iota((256, 256), 0) // 16
    from_j = iota((256, 256), 0) % 16
    to_slot = iota((256, 256), 1) // 16
    spread = onehot((from_slot == to_slot) & (from_j == PIECES))
    before = onehot((from_slot < to_slot) & (from_j == PIECES))
    right_piece = (row_j == HALF * col_h + col_j) & (col_j < HALF)

    for k, residue in enumerate((b + 3, b + 1, b + 2)):
        slot = z_buf.at[lax.rem(residue, 4)]
        remote(slot, slot, z2_send.at[k], z2_recv.at[k], at_z(1)).wait_recv()

    gathered = z_buf[...].reshape(256, PIECE)
    found = dot(expert_pick, gathered[:, :128], NT)
    found = jnp.where(row_j == PIECES, found, 0.0)
    taken = onehot(found > 0)
    slot_gate = dot(found.astype(BF16), spread)
    standing = dot(taken, before)
    chosen = (slot_gate > 0) & (standing == col_k.astype(F32)) & right_piece
    place = onehot(chosen)
    place_buf[...] = jnp.where(chosen, slot_gate, 0.0)
    x_send[...] = dot(place, gathered).astype(BF16).reshape(PEERS, 16, PIECE)
    for o in range(1, PEERS):
        to = lax.rem(me + o, PEERS)
        copy = remote(x_send.at[to], x_recv.at[me], x_ssem.at[o - 1], x_rsem.at[o - 1], peer(to))
        copy.start()
        sends.append(copy)
    x_recv[me] = x_send[me]

    context_ref[...] = dot(prob_buf[...], cache_buf[:, :LATENT]).astype(BF16)

    order_row = iota((HALF * ROWS, 128), 0)
    order_col = iota((HALF * ROWS, 128), 1)
    order = onehot(
        (order_row // 16 == order_col % 8)
        & (order_row % 16 // 2 == order_col // 16)
        & (order_row % 2 == order_col // 8 % 2)
    )
    for o in range(1, PEERS):
        slot = x_recv.at[lax.rem(me - o + PEERS, PEERS)]
        remote(slot, slot, x_ssem.at[o - 1], x_rsem.at[o - 1], peer(lax.rem(me + o, PEERS))).wait_recv()
    y_buf[0] = dot(order, x_recv[...].reshape(128, PIECE)).astype(BF16).reshape(HALF, ROWS, PIECE)

    def place_of(way, s):
        return 7 if s == 4 else 0 if s == 0 else 2 * s - 1 + way

    def gather(way, s, part):
        first, last = GROUPS[part]
        pieces = pl.ds(first, last - first)
        return remote(
            y_buf.at[place_of(way, s - 1), pieces], y_buf.at[place_of(way, s), pieces],
            y_ssem.at[way, s - 1, part], y_rsem.at[way, s - 1, part], at_y(1 - 2 * way),
        )

    def gather_wait(way, s, part):
        first, last = GROUPS[part]
        slot = y_buf.at[place_of(way, s), pl.ds(first, last - first)]
        remote(slot, slot, y_ssem.at[way, s - 1, part], y_rsem.at[way, s - 1, part], at_y(1 - 2 * way)).wait_recv()

    def project(first, last):
        rows = (last - first) * ROWS
        total = jnp.zeros((rows, 4 * HID), F32)
        for j in range(HALF):
            total += dot(
                y_buf[first:last, j].reshape(rows, PIECE),
                gu_buf[:, :, j * PIECE : (j + 1) * PIECE].reshape(4 * HID, PIECE),
                NT,
            )
        pre_buf[first * ROWS : last * ROWS, :] = total

    def exchange(k, first, last):
        rows = pl.ds(first * ROWS, (last - first) * ROWS)
        copy = remote(pre_buf.at[rows], pre_recv.at[rows], p_ssem.at[k], p_rsem.at[k], twin)
        copy.start()
        return copy

    def steps_of(s):
        return [(way, part) for part in range(2) for way in range(2) if s < 4 or part == way]

    for way, part in steps_of(1):
        copy = gather(way, 1, part)
        copy.start()
        sends.append(copy)
    for s in range(1, 4):
        for way, part in [(w, p) for p in range(2) for w in range(2)]:
            gather_wait(way, s, part)
            if (way, part) in steps_of(s + 1):
                copy = gather(way, s + 1, part)
                copy.start()
                sends.append(copy)
        if s == 1:
            for copy in own_copies[2:]:
                copy.wait()
            for k, (buf, slot) in enumerate(((gu_buf, other), (gu_buf, 2 + other), (down_buf, other))):
                ref = buf.at[slot]
                remote(ref, ref, w_send_sem.at[k], w_recv_sem.at[k], twin).wait_recv()
        if s == 2:
            project(0, 3)
        if s == 3:
            project(3, 7)
            exchanges = [exchange(0, 0, 7)]
    for way, part in steps_of(4):
        gather_wait(way, 4, part)
    project(7, 8)
    exchanges.append(exchange(1, 7, 8))
    for copy in exchanges:
        copy.wait_recv()
    sends += exchanges
    both = pre_buf[...] + pre_recv[...]
    gate_pre, up_pre = both[:, : 2 * HID], both[:, 2 * HID :]
    hidden = (gate_pre * jax.nn.sigmoid(gate_pre) * up_pre).astype(BF16)

    def down(part):
        for j in range(*GROUPS[part]):
            part_buf[:, j] = dot(
                hidden, down_buf[:, :, j * PIECE : (j + 1) * PIECE].reshape(2 * HID, PIECE)
            ).reshape(NY, ROWS, PIECE)

    def reduce_copy(way, s, part):
        first, last = GROUPS[part]
        pieces = pl.ds(first, last - first)
        return remote(
            rs_send.at[way, s - 1, pieces], rs_recv.at[way, s - 1, pieces],
            s_ssem.at[way, s - 1, part], s_rsem.at[way, s - 1, part], at_y(1 - 2 * way),
        )

    def reduce_send(way, s, part, received):
        first, last = GROUPS[part]
        total = part_buf[place_of(1 - way, 5 - s), first:last]
        if received:
            total = total + rs_recv[way, s - 2, first:last].astype(F32)
        rs_send[way, s - 1, first:last] = total.astype(BF16)
        copy = reduce_copy(way, s, part)
        copy.start()
        sends.append(copy)

    down(0)
    reduce_send(0, 1, 0, False)
    reduce_send(1, 2, 0, False)
    down(1)
    reduce_send(1, 1, 1, False)
    reduce_send(0, 2, 1, False)
    for s in range(2, 5):
        for part in range(2):
            for way in range(2):
                if s == 2 and part != way:
                    continue
                reduce_copy(way, s - 1, part).wait_recv()
                reduce_send(way, s, part, True)
    for part in range(2):
        first, last = GROUPS[part]
        for way in range(2):
            reduce_copy(way, 4, part).wait_recv()
            part_buf[0, first:last] += rs_recv[way, 3, first:last].astype(F32)

    back_row = iota((128, HALF * ROWS), 0)
    back_col = iota((128, HALF * ROWS), 1)
    back = onehot(
        (back_col // 16 == back_row % 8)
        & (back_col % 16 // 2 == back_row // 16)
        & (back_col % 2 == back_row // 8 % 2)
    )
    sums = part_buf[0].astype(BF16).reshape(HALF * ROWS, PIECE)
    b_send[...] = dot(back, sums).astype(BF16).reshape(PEERS, 16, PIECE)
    for o in range(1, PEERS):
        to = lax.rem(me + o, PEERS)
        copy = remote(b_send.at[to], b_recv.at[me], b_ssem.at[o - 1], b_rsem.at[o - 1], peer(to))
        copy.start()
        sends.append(copy)
    b_recv[me] = b_send[me]
    weigh = place_buf[...].T.astype(BF16)
    for o in range(1, PEERS):
        slot = b_recv.at[lax.rem(me - o + PEERS, PEERS)]
        remote(slot, slot, b_ssem.at[o - 1], b_rsem.at[o - 1], peer(lax.rem(me + o, PEERS))).wait_recv()

    c_buf[...] = dot(weigh, b_recv[...].reshape(128, PIECE)).astype(BF16).reshape(4, 4, 16, PIECE)
    for k, (step, residue) in enumerate(((1, b + 1), (-1, b + 3), (far, b + 2))):
        copy = remote(c_buf.at[lax.rem(residue, 4)], c_recv.at[k], c_ssem.at[k], c_rsem.at[k], at_z(step))
        copy.start()
        sends.append(copy)
    for k in range(3):
        remote(c_recv.at[k], c_recv.at[k], c_ssem.at[k], c_rsem.at[k], at_z(1)).wait_recv()
    near = c_buf[b].astype(F32)
    for k in range(3):
        near = near + c_recv[k].astype(F32)
    r_send[...] = near.astype(BF16)
    for o in range(1, 4):
        copy = remote(
            r_send.at[lax.rem(a + o, 4)], r_recv.at[o - 1], r_ssem.at[o - 1], r_rsem.at[o - 1], at_z(4 * o)
        )
        copy.start()
        sends.append(copy)
    total = r_send[a].astype(F32)
    for o in range(1, 4):
        remote(r_recv.at[o - 1], r_recv.at[o - 1], r_ssem.at[o - 1], r_rsem.at[o - 1], at_z(4 * o)).wait_recv()
        total = total + r_recv[o - 1].astype(F32)
    out_ref[...] = total.astype(BF16)
    for copy in sends:
        copy.wait_send()


def per_device(queries, latent_cache, lengths, moe_rows, expert_ids, route_gates, w_gate, w_up, w_down):
    picks = expert_ids[0][:, None] == jnp.arange(PIECE)[None, :]
    gates = jnp.sum(jnp.where(picks, route_gates[0][:, None].astype(F32), 0.0), axis=0)
    tail = jnp.stack([gates, jnp.zeros_like(gates)]).astype(BF16)
    block = jnp.concatenate([moe_rows.reshape(PIECES, PIECE), tail])

    any_spec = pl.BlockSpec(memory_space=pl.ANY)
    vmem_spec = pl.BlockSpec(memory_space=pltpu.VMEM)
    dma = pltpu.SemaphoreType.DMA
    context, out = pl.pallas_call(
        kernel,
        out_shape=(
            jax.ShapeDtypeStruct((HEADS, LATENT), BF16),
            jax.ShapeDtypeStruct((16, PIECE), BF16),
        ),
        in_specs=[pl.BlockSpec(memory_space=pltpu.SMEM), vmem_spec] + [any_spec] * 5,
        out_specs=(vmem_spec, vmem_spec),
        scratch_shapes=[
            pltpu.VMEM((HEADS, WIDTH), BF16),
            pltpu.VMEM((CTX, WIDTH), BF16),
            pltpu.VMEM((HEADS, CTX), F32),
            pltpu.VMEM((HEADS, CTX), BF16),
            pltpu.VMEM((4, HID, HALF_D), BF16),
            pltpu.VMEM((2, HID, HALF_D), BF16),
            pltpu.VMEM((4, 4, 16, PIECE), BF16),
            pltpu.VMEM((128, 256), F32),
            pltpu.VMEM((PEERS, 16, PIECE), BF16),
            pltpu.VMEM((PEERS, 16, PIECE), BF16),
            pltpu.VMEM((NY, HALF, ROWS, PIECE), BF16),
            pltpu.VMEM((128, 4 * HID), F32),
            pltpu.VMEM((128, 4 * HID), F32),
            pltpu.VMEM((NY, HALF, ROWS, PIECE), F32),
            pltpu.VMEM((2, 4, HALF, ROWS, PIECE), BF16),
            pltpu.VMEM((2, 4, HALF, ROWS, PIECE), BF16),
            pltpu.VMEM((PEERS, 16, PIECE), BF16),
            pltpu.VMEM((PEERS, 16, PIECE), BF16),
            pltpu.VMEM((4, 4, 16, PIECE), BF16),
            pltpu.VMEM((3, 4, 16, PIECE), BF16),
            pltpu.VMEM((4, 16, PIECE), BF16),
            pltpu.VMEM((3, 16, PIECE), BF16),
            dma((5,)), dma((3,)), dma((3,)),
            dma((3,)), dma((3,)), dma((3,)), dma((3,)),
            dma((7,)), dma((7,)),
            dma((2, 4, 2)), dma((2, 4, 2)),
            dma((2,)), dma((2,)),
            dma((2, 4, 2)), dma((2, 4, 2)),
            dma((7,)), dma((7,)),
            dma((3,)), dma((3,)), dma((3,)), dma((3,)),
        ],
        compiler_params=pltpu.CompilerParams(
            collective_id=0, has_side_effects=True, vmem_limit_bytes=40 * 1024 * 1024
        ),
        cost_estimate=pl.CostEstimate(flops=1_000_000_000, bytes_accessed=4_000_000, transcendentals=50_000),
    )(lengths, block, queries, latent_cache, w_gate, w_up, w_down)
    return context[None], out[:PIECES].reshape(1, D)


def solution(mesh):
    rows = P(("node", "local"), None)
    wide = P(("node", "local"), None, None)
    return jax.shard_map(
        per_device,
        mesh=mesh,
        in_specs=(wide, wide, P(("node", "local")), rows, rows, rows, wide, wide, wide),
        out_specs=(wide, rows),
        check_vma=False,
    )
```

```python
import jax
import jax.numpy as jnp
from jax import lax
from jax.experimental import pallas as pl
from jax.experimental.pallas import tpu as pltpu
from jax.sharding import PartitionSpec as P

MESH = pl.DeviceIdType.MESH
BF16, F32 = jnp.bfloat16, jnp.float32

D = 7168
HEADS = 128
CTX = 320
WIDTH = 576
LATENT = 512
HID = 64
EXPERTS = 64
E_NODE = 4
NZ, NX, NY, NC = 16, 4, 8, 2
PEERS = NX * NC
PIECE = 512
PIECES = D // PIECE
HALF = PIECES // 2
HALF_D = D // 2
ROWS = 16
GROUPS = ((0, 4), (4, 7))
SCALE = 192.0**-0.5


def iota(shape, dim):
    return lax.broadcasted_iota(jnp.int32, shape, dim)


def onehot(condition):
    return jnp.where(condition, 1.0, 0.0).astype(BF16)


def dot(a, b, dims=((1,), (0,))):
    return lax.dot_general(a, b, (dims, ((), ())), preferred_element_type=F32)


NT = ((1,), (1,))
TN = ((0,), (0,))


def kernel(
    length_ref, row_ref, id_ref, gate_ref, q_hbm, cache_hbm, gate_hbm, up_hbm, down_hbm,
    context_ref, out_ref,
    q_buf, cache_buf, score_buf, prob_buf, gu_buf, down_buf,
    z_buf, place_buf, x_send, x_recv, y_buf, pre_mid, mid_recv, pre_end, end_recv, part_buf,
    rs_send, rs_recv, b_send, b_recv, c_buf, c_recv, r_send, r_recv, filler,
    in_sem, w_send_sem, w_recv_sem, z1_send, z1_recv, z2_send, z2_recv,
    x_ssem, x_rsem, y_ssem, y_rsem, p_ssem, p_rsem,
    s_ssem, s_rsem, b_ssem, b_rsem, c_ssem, c_rsem, r_ssem, r_rsem,
):
    g = lax.axis_index("node")
    l = lax.axis_index("local")
    x, y, c = l // 16, (l % 16) // 2, l % 2
    a, b = g // 4, g % 4
    me = x * NC + c
    other = 1 - c

    def at_z(step):
        return (lax.rem(g + step + NZ, NZ), l)

    def at_y(step):
        return (g, x * 16 + lax.rem(y + step + NY, NY) * 2 + c)

    def peer(n):
        return (g, (n // NC) * 16 + y * 2 + n % NC)

    twin = (g, l + 1 - 2 * c)

    def remote(src, dst, ssem, rsem, device):
        return pltpu.make_async_remote_copy(
            src_ref=src, dst_ref=dst, send_sem=ssem, recv_sem=rsem,
            device_id=device, device_id_type=MESH,
        )

    mine = pl.ds(pl.multiple_of(c * HALF_D, 128), HALF_D)
    theirs = pl.ds(pl.multiple_of(other * HALF_D, 128), HALF_D)
    own_copies = [
        pltpu.make_async_copy(q_hbm.at[0], q_buf, in_sem.at[0]),
        pltpu.make_async_copy(cache_hbm.at[0], cache_buf, in_sem.at[1]),
        pltpu.make_async_copy(gate_hbm.at[0, :, mine], gu_buf.at[c], in_sem.at[2]),
        pltpu.make_async_copy(up_hbm.at[0, :, mine], gu_buf.at[2 + c], in_sem.at[3]),
        pltpu.make_async_copy(down_hbm.at[0, :, mine], down_buf.at[c], in_sem.at[4]),
    ]
    for copy in own_copies:
        copy.start()
    sends = []

    barrier = pltpu.get_barrier_semaphore()
    z_steps = (1, -1, 2, -2, 4, 8, 12)
    partners = [at_z(s) for s in z_steps]
    partners += [peer(lax.rem(me + o, PEERS)) for o in range(1, PEERS)]
    partners += [at_y(1), at_y(-1)]
    for device in partners:
        pl.semaphore_signal(barrier, inc=1, device_id=device, device_id_type=MESH)
    lane = iota((1, PIECE), 1)
    gates = jnp.zeros((1, PIECE), F32)
    for k in range(8):
        gates = gates + jnp.where(lane == id_ref[:, k : k + 1], gate_ref[:, k : k + 1].astype(F32), 0.0)
    pieces = [row_ref[:, j * PIECE : (j + 1) * PIECE].astype(F32) for j in range(PIECES)]
    z_buf[b, a] = jnp.concatenate(pieces + [gates, jnp.zeros((1, PIECE), F32)], axis=0).astype(BF16)
    pl.semaphore_wait(barrier, len(partners))

    for o in (2, 1, 3):
        copy = remote(z_buf.at[b, a], z_buf.at[b, a], z1_send.at[o - 1], z1_recv.at[o - 1], at_z(4 * o))
        copy.start()
        sends.append(copy)
    far = 4 * (g % 2) - 2
    near_steps = (1, -1, far)

    def hand_on(o):
        slot = z_buf.at[b, lax.rem(a - o + 4, 4)]
        for k, step in enumerate(near_steps):
            copy = remote(slot, slot, z2_send.at[k, o], z2_recv.at[k, o], at_z(step))
            copy.start()
            sends.append(copy)

    hand_on(0)
    for k, (hbm, buf, slot) in enumerate(
        ((gate_hbm, gu_buf, c), (up_hbm, gu_buf, 2 + c), (down_hbm, down_buf, c))
    ):
        copy = remote(hbm.at[0, :, theirs], buf.at[slot], w_send_sem.at[k], w_recv_sem.at[k], twin)
        copy.start()
        sends.append(copy)

    own_copies[0].wait()
    own_copies[1].wait()
    score_buf[...] = dot(cache_buf[...], q_buf[...]) * SCALE
    visible = iota((CTX, HEADS), 0) < length_ref[0]
    scores = jnp.where(visible, score_buf[...], -1e30)
    highest = jnp.max(scores, axis=0, keepdims=True)
    weights = jnp.where(visible, jnp.exp(scores - highest), 0.0)
    prob_buf[...] = (weights / jnp.sum(weights, axis=0, keepdims=True)).astype(BF16)

    column = iota((128, 256), 0)
    col_j = column & 7
    row_j = iota((128, 256), 1) & 15
    expert_pick = onehot(iota((128, 128), 1) == E_NODE * g + (iota((128, 128), 0) >> 5))
    from_row = iota((256, 256), 0)
    from_slot, from_tail = from_row >> 4, (from_row & 15) == PIECES
    to_slot = iota((256, 256), 1) >> 4
    spread = onehot((from_slot == to_slot) & from_tail)
    before = onehot((from_slot < to_slot) & from_tail)
    right_piece = (row_j == HALF * (column >> 4 & 1) + col_j) & (col_j < HALF)
    wanted_standing = (column >> 3 & 1).astype(F32)

    order_row = iota((HALF * ROWS, 128), 0)
    order_col = iota((HALF * ROWS, 128), 1)
    order = onehot(
        (order_row >> 4 == (order_col & 7))
        & ((order_row & 15) >> 1 == order_col >> 4)
        & ((order_row & 1) == (order_col >> 3 & 1))
    )

    pre_mid[...] = jnp.zeros_like(pre_mid)

    for o in (1, 3, 2):
        slot = z_buf.at[b, lax.rem(a - o + 4, 4)]
        remote(slot, slot, z1_send.at[o - 1], z1_recv.at[o - 1], at_z(4 * o)).wait_recv()
        hand_on(o)

    context_ref[...] = dot(prob_buf[...], cache_buf[:, :LATENT], TN).astype(BF16)

    for o in (0, 1, 3, 2):
        for k, step in enumerate(near_steps):
            plane = lax.rem(g - step + NZ, NZ)
            slot = z_buf.at[plane % 4, lax.rem(plane // 4 - o + 4, 4)]
            remote(slot, slot, z2_send.at[k, o], z2_recv.at[k, o], at_z(step)).wait_recv()
    gathered = z_buf[...].reshape(256, PIECE)
    found = dot(expert_pick, gathered[:, :128], NT)
    found = jnp.where(row_j == PIECES, found, 0.0)
    taken = onehot(found > 0)
    slot_gate = dot(found.astype(BF16), spread)
    standing = dot(taken, before)
    chosen = (slot_gate > 0) & (standing == wanted_standing) & right_piece
    place = onehot(chosen)
    place_buf[...] = jnp.where(chosen, slot_gate, 0.0)
    x_send[...] = dot(place, gathered).astype(BF16).reshape(PEERS, 16, PIECE)
    for o in range(1, PEERS):
        to = lax.rem(me + o, PEERS)
        copy = remote(x_send.at[to], x_recv.at[me], x_ssem.at[o - 1], x_rsem.at[o - 1], peer(to))
        copy.start()
        sends.append(copy)
    x_recv[me] = x_send[me]

    for o in range(1, PEERS):
        slot = x_recv.at[lax.rem(me - o + PEERS, PEERS)]
        remote(slot, slot, x_ssem.at[o - 1], x_rsem.at[o - 1], peer(lax.rem(me + o, PEERS))).wait_recv()
    y_buf[0] = dot(order, x_recv[...].reshape(128, PIECE)).astype(BF16).reshape(HALF, ROWS, PIECE)

    def place_of(way, s):
        return 7 if s == 4 else 0 if s == 0 else 2 * s - 1 + way

    def gather(way, s, j):
        return remote(
            y_buf.at[place_of(way, s - 1), j], y_buf.at[place_of(way, s), j],
            y_ssem.at[way, s - 1, j], y_rsem.at[way, s - 1, j], at_y(1 - 2 * way),
        )

    def gather_wait(way, s, j):
        slot = y_buf.at[place_of(way, s), j]
        remote(slot, slot, y_ssem.at[way, s - 1, j], y_rsem.at[way, s - 1, j], at_y(1 - 2 * way)).wait_recv()

    def weight_piece(j):
        return gu_buf[:, :, j * PIECE : (j + 1) * PIECE].reshape(4 * HID, PIECE)

    last_way = [0] * GROUPS[0][1] + [1] * (HALF - GROUPS[0][1])

    def steps_of(s):
        return [(way, j) for j in range(HALF) for way in range(2) if s < 4 or last_way[j] == way]

    for way, j in steps_of(1):
        copy = gather(way, 1, j)
        copy.start()
        sends.append(copy)
    for s in range(1, 4):
        for way, j in steps_of(s):
            gather_wait(way, s, j)
            if (way, j) in steps_of(s + 1):
                copy = gather(way, s + 1, j)
                copy.start()
                sends.append(copy)
        if s == 1:
            for copy in own_copies[2:]:
                copy.wait()
            for k, (buf, slot) in enumerate(((gu_buf, other), (gu_buf, 2 + other), (down_buf, other))):
                ref = buf.at[slot]
                remote(ref, ref, w_send_sem.at[k], w_recv_sem.at[k], twin).wait_recv()
        if s == 3:
            rows = 7 * ROWS
            total = jnp.zeros((4 * HID, rows), F32)
            for j in range(HALF):
                total += dot(weight_piece(j), y_buf[:7, j].reshape(rows, PIECE), NT)
            pre_mid[:, :rows] = total
            mid = remote(pre_mid, mid_recv, p_ssem.at[0], p_rsem.at[0], twin)
            mid.start()
            sends.append(mid)
    for way, j in steps_of(4):
        gather_wait(way, 4, j)
    total = jnp.zeros((ROWS, 4 * HID), F32)
    for j in range(HALF):
        total += dot(y_buf[7, j], weight_piece(j), NT)
    pre_end[...] = total
    end = remote(pre_end, end_recv, p_ssem.at[1], p_rsem.at[1], twin)
    end.start()
    sends.append(end)

    def down(hidden, j):
        return dot(hidden, down_buf[:, :, j * PIECE : (j + 1) * PIECE].reshape(2 * HID, PIECE))

    def reduce_copy(way, s, j):
        return remote(
            rs_send.at[way, s - 1, j], rs_recv.at[way, s - 1, j],
            s_ssem.at[way, s - 1, j], s_rsem.at[way, s - 1, j], at_y(1 - 2 * way),
        )

    def reduce_send(way, s, j, received):
        total = part_buf[place_of(1 - way, 5 - s), j]
        if received:
            total = total + rs_recv[way, s - 2, j].astype(F32)
        rs_send[way, s - 1, j] = total.astype(BF16)
        copy = reduce_copy(way, s, j)
        copy.start()
        sends.append(copy)

    mid.wait_recv()
    both = pre_mid[...] + mid_recv[...]
    gate_pre, up_pre = both[: 2 * HID], both[2 * HID :]
    hidden = (gate_pre * jax.nn.sigmoid(gate_pre) * up_pre).T[: 7 * ROWS].astype(BF16)
    turns = [j for pair in zip(range(4), (4, 5, 6, None)) for j in pair if j is not None]
    for j in turns:
        part_buf[:, j] = down(hidden, j).reshape(7, ROWS, PIECE)
        reduce_send(1 - last_way[j], 2, j, False)
    end.wait_recv()
    both = pre_end[...] + end_recv[...]
    gate_pre, up_pre = both[:, : 2 * HID], both[:, 2 * HID :]
    hidden = (gate_pre * jax.nn.sigmoid(gate_pre) * up_pre).astype(BF16)
    for j in turns:
        way = last_way[j]
        rs_send[way, 0, j] = down(hidden, j).astype(BF16)
        copy = reduce_copy(way, 1, j)
        copy.start()
        sends.append(copy)
    for j in turns:
        way = last_way[j]
        reduce_copy(way, 1, j).wait_recv()
        reduce_send(way, 2, j, True)
    early = [(1 - last_way[j], j) for j in turns] + [(last_way[j], j) for j in turns]
    for s in range(3, 5):
        for way, j in early:
            reduce_copy(way, s - 1, j).wait_recv()
            reduce_send(way, s, j, True)
    for way, j in early:
        reduce_copy(way, 4, j).wait_recv()
        part_buf[0, j] += rs_recv[way, 3, j].astype(F32)

    sums = part_buf[0].astype(BF16).reshape(HALF * ROWS, PIECE)
    b_send[...] = dot(order, sums, TN).astype(BF16).reshape(PEERS, 16, PIECE)
    for o in range(1, PEERS):
        to = lax.rem(me + o, PEERS)
        copy = remote(b_send.at[to], b_recv.at[me], b_ssem.at[o - 1], b_rsem.at[o - 1], peer(to))
        copy.start()
        sends.append(copy)
    b_recv[me] = b_send[me]
    weigh = place_buf[...].T.astype(BF16)
    for o in range(1, PEERS):
        slot = b_recv.at[lax.rem(me - o + PEERS, PEERS)]
        remote(slot, slot, b_ssem.at[o - 1], b_rsem.at[o - 1], peer(lax.rem(me + o, PEERS))).wait_recv()

    c_buf[...] = dot(weigh, b_recv[...].reshape(128, PIECE)).astype(BF16).reshape(4, 4, 16, PIECE)
    for o in (2, 1, 3, 0):
        for k, step in enumerate(near_steps):
            plane = lax.rem(g + step + NZ, NZ)
            copy = remote(
                c_buf.at[plane % 4, lax.rem(plane // 4 + o, 4)], c_recv.at[k, o],
                c_ssem.at[k, o], c_rsem.at[k, o], at_z(step),
            )
            copy.start()
            sends.append(copy)
    for o in (2, 1, 3, 0):
        total = c_buf[b, lax.rem(a + o, 4)].astype(F32)
        for k in range(3):
            remote(c_recv.at[k, o], c_recv.at[k, o], c_ssem.at[k, o], c_rsem.at[k, o], at_z(1)).wait_recv()
            total = total + c_recv[k, o].astype(F32)
        if o > 0:
            r_send[o - 1] = total.astype(BF16)
            copy = remote(r_send.at[o - 1], r_recv.at[o - 1], r_ssem.at[o - 1], r_rsem.at[o - 1], at_z(4 * o))
            copy.start()
            sends.append(copy)
    for o in (1, 3, 2):
        remote(r_recv.at[o - 1], r_recv.at[o - 1], r_ssem.at[o - 1], r_rsem.at[o - 1], at_z(4 * o)).wait_recv()
        total = total + r_recv[o - 1].astype(F32)
    for j in range(PIECES):
        out_ref[:, j * PIECE : (j + 1) * PIECE] = total[j : j + 1].astype(BF16)
    for copy in sends:
        copy.wait_send()


def per_device(queries, latent_cache, lengths, moe_rows, expert_ids, route_gates, w_gate, w_up, w_down):
    any_spec = pl.BlockSpec(memory_space=pl.ANY)
    vmem_spec = pl.BlockSpec(memory_space=pltpu.VMEM)
    dma = pltpu.SemaphoreType.DMA
    context, out = pl.pallas_call(
        kernel,
        out_shape=(
            jax.ShapeDtypeStruct((HEADS, LATENT), BF16),
            jax.ShapeDtypeStruct((1, D), BF16),
        ),
        in_specs=[pl.BlockSpec(memory_space=pltpu.SMEM)] + [vmem_spec] * 3 + [any_spec] * 5,
        out_specs=(vmem_spec, vmem_spec),
        scratch_shapes=[
            pltpu.VMEM((WIDTH, HEADS), BF16),
            pltpu.VMEM((CTX, WIDTH), BF16),
            pltpu.VMEM((CTX, HEADS), F32),
            pltpu.VMEM((CTX, HEADS), BF16),
            pltpu.VMEM((4, HID, HALF_D), BF16),
            pltpu.VMEM((2, HID, HALF_D), BF16),
            pltpu.VMEM((4, 4, 16, PIECE), BF16),
            pltpu.VMEM((128, 256), F32),
            pltpu.VMEM((PEERS, 16, PIECE), BF16),
            pltpu.VMEM((PEERS, 16, PIECE), BF16),
            pltpu.VMEM((NY, HALF, ROWS, PIECE), BF16),
            pltpu.VMEM((4 * HID, 128), F32),
            pltpu.VMEM((4 * HID, 128), F32),
            pltpu.VMEM((ROWS, 4 * HID), F32),
            pltpu.VMEM((ROWS, 4 * HID), F32),
            pltpu.VMEM((NY - 1, HALF, ROWS, PIECE), F32),
            pltpu.VMEM((2, 4, HALF, ROWS, PIECE), BF16),
            pltpu.VMEM((2, 4, HALF, ROWS, PIECE), BF16),
            pltpu.VMEM((PEERS, 16, PIECE), BF16),
            pltpu.VMEM((PEERS, 16, PIECE), BF16),
            pltpu.VMEM((4, 4, 16, PIECE), BF16),
            pltpu.VMEM((3, 4, 16, PIECE), BF16),
            pltpu.VMEM((3, 16, PIECE), BF16),
            pltpu.VMEM((3, 16, PIECE), BF16),
            pltpu.VMEM((2880, 8192), BF16),
            dma((5,)), dma((3,)), dma((3,)),
            dma((3,)), dma((3,)), dma((3, 4)), dma((3, 4)),
            dma((7,)), dma((7,)),
            dma((2, 4, 7)), dma((2, 4, 7)),
            dma((2,)), dma((2,)),
            dma((2, 4, 7)), dma((2, 4, 7)),
            dma((7,)), dma((7,)),
            dma((3, 4)), dma((3, 4)), dma((3,)), dma((3,)),
        ],
        compiler_params=pltpu.CompilerParams(
            collective_id=0, has_side_effects=True, vmem_limit_bytes=60 * 1024 * 1024
        ),
        cost_estimate=pl.CostEstimate(flops=1_000_000_000, bytes_accessed=4_000_000, transcendentals=50_000),
    )(lengths, moe_rows, expert_ids, route_gates, jnp.swapaxes(queries, 1, 2), latent_cache, w_gate, w_up, w_down)
    return context[None], out


def solution(mesh):
    rows = P(("node", "local"), None)
    wide = P(("node", "local"), None, None)
    return jax.shard_map(
        per_device,
        mesh=mesh,
        in_specs=(wide, wide, P(("node", "local")), rows, rows, rows, wide, wide, wide),
        out_specs=(wide, rows),
        check_vma=False,
    )
```

```python
import jax
import jax.numpy as jnp
from jax import lax
from jax.experimental import pallas as pl
from jax.experimental.pallas import tpu as pltpu
from jax.sharding import PartitionSpec as P

MESH = pl.DeviceIdType.MESH
BF16, F32 = jnp.bfloat16, jnp.float32

D = 7168
HEADS = 128
CTX = 320
WIDTH = 576
LATENT = 512
HID = 64
EXPERTS = 64
E_NODE = 4
NZ, NX, NY, NC = 16, 4, 8, 2
PEERS = NX * NC
PIECE = 512
PIECES = D // PIECE
LANES = PIECE // 2
HALF = PIECES // 2
HALF_D = D // 2
ROWS = 16
GROUPS = ((0, 4), (4, 7))
SCALE = 192.0**-0.5


def iota(shape, dim):
    return lax.broadcasted_iota(jnp.int32, shape, dim)


def onehot(condition):
    return jnp.where(condition, 1.0, 0.0).astype(BF16)


def dot(a, b, dims=((1,), (0,))):
    return lax.dot_general(a, b, (dims, ((), ())), preferred_element_type=F32)


NT = ((1,), (1,))
TN = ((0,), (0,))


def kernel(
    length_ref, row_ref, id_ref, gate_ref, q_hbm, cache_hbm, gate_hbm, up_hbm, down_hbm,
    context_ref, out_ref,
    q_buf, cache_buf, score_buf, prob_buf, gu_buf, down_buf,
    z_buf, place_buf, x_send, x_recv, y_buf, pre_mid, mid_recv, pre_end, end_recv, part_buf,
    rs_send, rs_recv, b_send, b_recv, c_buf, c_recv, r_send, r_recv,
    in_sem, w_send_sem, w_recv_sem, z1_send, z1_recv, z2_send, z2_recv,
    x_ssem, x_rsem, y_ssem, y_rsem, p_ssem, p_rsem,
    s_ssem, s_rsem, b_ssem, b_rsem, c_ssem, c_rsem, r_ssem, r_rsem,
):
    g = lax.axis_index("node")
    l = lax.axis_index("local")
    x, y, c = l // 16, (l % 16) // 2, l % 2
    a, b = g // 4, g % 4
    me = x * NC + c
    other = 1 - c

    def at_z(step):
        return (lax.rem(g + step + NZ, NZ), l)

    def at_y(step):
        return (g, x * 16 + lax.rem(y + step + NY, NY) * 2 + c)

    def peer(n):
        return (g, (n // NC) * 16 + y * 2 + n % NC)

    twin = (g, l + 1 - 2 * c)

    def remote(src, dst, ssem, rsem, device):
        return pltpu.make_async_remote_copy(
            src_ref=src, dst_ref=dst, send_sem=ssem, recv_sem=rsem,
            device_id=device, device_id_type=MESH,
        )

    mine = pl.ds(pl.multiple_of(c * HALF_D, 128), HALF_D)
    theirs = pl.ds(pl.multiple_of(other * HALF_D, 128), HALF_D)
    own_copies = [
        pltpu.make_async_copy(q_hbm.at[0], q_buf, in_sem.at[0]),
        pltpu.make_async_copy(cache_hbm.at[0], cache_buf, in_sem.at[1]),
        pltpu.make_async_copy(gate_hbm.at[0, :, mine], gu_buf.at[c], in_sem.at[2]),
        pltpu.make_async_copy(up_hbm.at[0, :, mine], gu_buf.at[2 + c], in_sem.at[3]),
        pltpu.make_async_copy(down_hbm.at[0, :, mine], down_buf.at[c], in_sem.at[4]),
    ]
    for copy in own_copies:
        copy.start()
    sends = []

    barrier = pltpu.get_barrier_semaphore()
    z_steps = (1, -1, 2, -2, 4, 8, 12)
    partners = [at_z(s) for s in z_steps]
    partners += [peer(lax.rem(me + o, PEERS)) for o in range(1, PEERS)]
    partners += [at_y(1), at_y(-1)]
    for device in partners:
        pl.semaphore_signal(barrier, inc=1, device_id=device, device_id_type=MESH)
    lane = iota((1, PIECE), 1)
    gates = jnp.zeros((1, PIECE), F32)
    for k in range(8):
        gates = gates + jnp.where(lane == id_ref[:, k : k + 1], gate_ref[:, k : k + 1].astype(F32), 0.0)
    pieces = [row_ref[:, j * PIECE : (j + 1) * PIECE].astype(F32) for j in range(PIECES)]
    block = jnp.concatenate(pieces + [gates, jnp.zeros((1, PIECE), F32)], axis=0).astype(BF16)
    for q in range(2):
        z_buf[q, b, a] = block[:, q * LANES : (q + 1) * LANES]
    pl.semaphore_wait(barrier, len(partners))

    far = 4 * (g % 2) - 2
    near_steps = (1, -1, far)

    def hand_on(q, o):
        slot = z_buf.at[q, b, lax.rem(a - o + 4, 4)]
        for k, step in enumerate(near_steps):
            copy = remote(slot, slot, z2_send.at[q, k, o], z2_recv.at[q, k, o], at_z(step))
            copy.start()
            sends.append(copy)

    for q in range(2):
        slot = z_buf.at[q, b, a]
        for o in (2, 1, 3):
            copy = remote(slot, slot, z1_send.at[q, o - 1], z1_recv.at[q, o - 1], at_z(4 * o))
            copy.start()
            sends.append(copy)
        hand_on(q, 0)
    for k, (hbm, buf, slot) in enumerate(
        ((gate_hbm, gu_buf, c), (up_hbm, gu_buf, 2 + c), (down_hbm, down_buf, c))
    ):
        copy = remote(hbm.at[0, :, theirs], buf.at[slot], w_send_sem.at[k], w_recv_sem.at[k], twin)
        copy.start()
        sends.append(copy)

    column = iota((128, 256), 0)
    col_j = column & 7
    row_j = iota((128, 256), 1) & 15
    expert_pick = onehot(iota((128, 128), 1) == E_NODE * g + (iota((128, 128), 0) >> 5))
    from_row = iota((256, 256), 0)
    from_slot, from_tail = from_row >> 4, (from_row & 15) == PIECES
    to_slot = iota((256, 256), 1) >> 4
    spread = onehot((from_slot == to_slot) & from_tail)
    before = onehot((from_slot < to_slot) & from_tail)
    right_piece = (row_j == HALF * (column >> 4 & 1) + col_j) & (col_j < HALF)
    wanted_standing = (column >> 3 & 1).astype(F32)

    order_row = iota((HALF * ROWS, 128), 0)
    order_col = iota((HALF * ROWS, 128), 1)
    order = onehot(
        (order_row >> 4 == (order_col & 7))
        & ((order_row & 15) >> 1 == order_col >> 4)
        & ((order_row & 1) == (order_col >> 3 & 1))
    )

    pre_mid[...] = jnp.zeros_like(pre_mid)

    for q in range(2):
        for o in (1, 3, 2):
            slot = z_buf.at[q, b, lax.rem(a - o + 4, 4)]
            remote(slot, slot, z1_send.at[q, o - 1], z1_recv.at[q, o - 1], at_z(4 * o)).wait_recv()
            hand_on(q, o)

    for q in range(2):
        for o in (0, 1, 3, 2):
            for k, step in enumerate(near_steps):
                plane = lax.rem(g - step + NZ, NZ)
                slot = z_buf.at[q, plane % 4, lax.rem(plane // 4 - o + 4, 4)]
                remote(slot, slot, z2_send.at[q, k, o], z2_recv.at[q, k, o], at_z(step)).wait_recv()
        gathered = z_buf[q].reshape(256, LANES)
        if q == 0:
            found = dot(expert_pick, gathered[:, :128], NT)
            found = jnp.where(row_j == PIECES, found, 0.0)
            taken = onehot(found > 0)
            slot_gate = dot(found.astype(BF16), spread)
            standing = dot(taken, before)
            chosen = (slot_gate > 0) & (standing == wanted_standing) & right_piece
            place = onehot(chosen)
            place_buf[...] = jnp.where(chosen, slot_gate, 0.0)
        x_send[q] = dot(place, gathered).astype(BF16).reshape(PEERS, 16, LANES)
        for o in range(1, PEERS):
            to = lax.rem(me + o, PEERS)
            copy = remote(x_send.at[q, to], x_recv.at[q, me], x_ssem.at[q, o - 1], x_rsem.at[q, o - 1], peer(to))
            copy.start()
            sends.append(copy)
        x_recv[q, me] = x_send[q, me]

    def place_of(way, s):
        return 7 if s == 4 else 0 if s == 0 else 2 * s - 1 + way

    def gather(way, s, q, part):
        first, last = GROUPS[part]
        pieces = pl.ds(first, last - first)
        return remote(
            y_buf.at[place_of(way, s - 1), q, pieces], y_buf.at[place_of(way, s), q, pieces],
            y_ssem.at[way, s - 1, q, part], y_rsem.at[way, s - 1, q, part], at_y(1 - 2 * way),
        )

    def gather_wait(way, s, q, part):
        first, last = GROUPS[part]
        slot = y_buf.at[place_of(way, s), q, pl.ds(first, last - first)]
        ssem, rsem = y_ssem.at[way, s - 1, q, part], y_rsem.at[way, s - 1, q, part]
        remote(slot, slot, ssem, rsem, at_y(1 - 2 * way)).wait_recv()

    def weight_piece(q, j):
        first = j * PIECE + q * LANES
        return gu_buf[:, :, first : first + LANES].reshape(4 * HID, LANES)

    last_way = [0] * GROUPS[0][1] + [1] * (HALF - GROUPS[0][1])

    def steps_of(s, q):
        return [(way, q, part) for part in range(2) for way in range(2) if s < 4 or part == way]

    for q in range(2):
        for o in range(1, PEERS):
            slot = x_recv.at[q, lax.rem(me - o + PEERS, PEERS)]
            to = peer(lax.rem(me + o, PEERS))
            remote(slot, slot, x_ssem.at[q, o - 1], x_rsem.at[q, o - 1], to).wait_recv()
        y_buf[0, q] = dot(order, x_recv[q].reshape(128, LANES)).astype(BF16).reshape(HALF, ROWS, LANES)
        for chunk in steps_of(1, q):
            copy = gather(chunk[0], 1, *chunk[1:])
            copy.start()
            sends.append(copy)
    for s in range(1, 4):
        for q in range(2):
            for way, _, part in steps_of(s, q):
                gather_wait(way, s, q, part)
                if s < 3 or part == way:
                    copy = gather(way, s + 1, q, part)
                    copy.start()
                    sends.append(copy)
        if s == 1:
            for copy in own_copies[2:]:
                copy.wait()
            for k, (buf, slot) in enumerate(((gu_buf, other), (gu_buf, 2 + other), (down_buf, other))):
                ref = buf.at[slot]
                remote(ref, ref, w_send_sem.at[k], w_recv_sem.at[k], twin).wait_recv()
        if s == 3:
            rows = 7 * ROWS
            total = jnp.zeros((4 * HID, rows), F32)
            for q in range(2):
                for j in range(HALF):
                    total += dot(weight_piece(q, j), y_buf[:7, q, j].reshape(rows, LANES), NT)
            pre_mid[:, :rows] = total
            mid = remote(pre_mid, mid_recv, p_ssem.at[0], p_rsem.at[0], twin)
            mid.start()
            sends.append(mid)
    for q in range(2):
        for way, _, part in steps_of(4, q):
            gather_wait(way, 4, q, part)
    total = jnp.zeros((ROWS, 4 * HID), F32)
    for q in range(2):
        for j in range(HALF):
            total += dot(y_buf[7, q, j], weight_piece(q, j), NT)
    pre_end[...] = total
    end = remote(pre_end, end_recv, p_ssem.at[1], p_rsem.at[1], twin)
    end.start()
    sends.append(end)

    def down(hidden, j):
        return dot(hidden, down_buf[:, :, j * PIECE : (j + 1) * PIECE].reshape(2 * HID, PIECE))

    def reduce_copy(way, s, j):
        return remote(
            rs_send.at[way, s - 1, j], rs_recv.at[way, s - 1, j],
            s_ssem.at[way, s - 1, j], s_rsem.at[way, s - 1, j], at_y(1 - 2 * way),
        )

    def reduce_send(way, s, j, received):
        total = part_buf[place_of(1 - way, 5 - s), j]
        if received:
            total = total + rs_recv[way, s - 2, j].astype(F32)
        rs_send[way, s - 1, j] = total.astype(BF16)
        copy = reduce_copy(way, s, j)
        copy.start()
        sends.append(copy)

    mid.wait_recv()
    both = pre_mid[...] + mid_recv[...]
    gate_pre, up_pre = both[: 2 * HID], both[2 * HID :]
    hidden = (gate_pre * jax.nn.sigmoid(gate_pre) * up_pre).T[: 7 * ROWS].astype(BF16)
    turns = [j for pair in zip(range(4), (4, 5, 6, None)) for j in pair if j is not None]
    for j in turns:
        part_buf[:, j] = down(hidden, j).reshape(7, ROWS, PIECE)
        reduce_send(1 - last_way[j], 2, j, False)
    end.wait_recv()
    both = pre_end[...] + end_recv[...]
    gate_pre, up_pre = both[:, : 2 * HID], both[:, 2 * HID :]
    hidden = (gate_pre * jax.nn.sigmoid(gate_pre) * up_pre).astype(BF16)
    for j in turns:
        way = last_way[j]
        rs_send[way, 0, j] = down(hidden, j).astype(BF16)
        copy = reduce_copy(way, 1, j)
        copy.start()
        sends.append(copy)
    for j in turns:
        way = last_way[j]
        reduce_copy(way, 1, j).wait_recv()
        reduce_send(way, 2, j, True)
    early = [(1 - last_way[j], j) for j in turns] + [(last_way[j], j) for j in turns]
    for s in range(3, 5):
        for way, j in early:
            reduce_copy(way, s - 1, j).wait_recv()
            reduce_send(way, s, j, True)
    for way, j in early:
        reduce_copy(way, 4, j).wait_recv()
        part_buf[0, j] += rs_recv[way, 3, j].astype(F32)

    sums = part_buf[0].astype(BF16).reshape(HALF * ROWS, PIECE)
    b_send[...] = dot(order, sums, TN).astype(BF16).reshape(PEERS, 16, PIECE)
    for o in range(1, PEERS):
        to = lax.rem(me + o, PEERS)
        copy = remote(b_send.at[to], b_recv.at[me], b_ssem.at[o - 1], b_rsem.at[o - 1], peer(to))
        copy.start()
        sends.append(copy)
    b_recv[me] = b_send[me]
    own_copies[0].wait()
    own_copies[1].wait()
    score_buf[...] = dot(cache_buf[...], q_buf[...]) * SCALE
    visible = iota((CTX, HEADS), 0) < length_ref[0]
    scores = jnp.where(visible, score_buf[...], -1e30)
    highest = jnp.max(scores, axis=0, keepdims=True)
    weights = jnp.where(visible, jnp.exp(scores - highest), 0.0)
    prob_buf[...] = (weights / jnp.sum(weights, axis=0, keepdims=True)).astype(BF16)

    weigh = place_buf[...].T.astype(BF16)
    for o in range(1, PEERS):
        slot = b_recv.at[lax.rem(me - o + PEERS, PEERS)]
        remote(slot, slot, b_ssem.at[o - 1], b_rsem.at[o - 1], peer(lax.rem(me + o, PEERS))).wait_recv()

    c_buf[...] = dot(weigh, b_recv[...].reshape(128, PIECE)).astype(BF16).reshape(4, 4, 16, PIECE)
    for o in (2, 1, 3, 0):
        for k, step in enumerate(near_steps):
            plane = lax.rem(g + step + NZ, NZ)
            copy = remote(
                c_buf.at[plane % 4, lax.rem(plane // 4 + o, 4)], c_recv.at[k, o],
                c_ssem.at[k, o], c_rsem.at[k, o], at_z(step),
            )
            copy.start()
            sends.append(copy)
    context_ref[...] = dot(prob_buf[...], cache_buf[:, :LATENT], TN).astype(BF16)

    for o in (2, 1, 3, 0):
        total = c_buf[b, lax.rem(a + o, 4)].astype(F32)
        for k in range(3):
            remote(c_recv.at[k, o], c_recv.at[k, o], c_ssem.at[k, o], c_rsem.at[k, o], at_z(1)).wait_recv()
            total = total + c_recv[k, o].astype(F32)
        if o > 0:
            r_send[o - 1] = total.astype(BF16)
            copy = remote(r_send.at[o - 1], r_recv.at[o - 1], r_ssem.at[o - 1], r_rsem.at[o - 1], at_z(4 * o))
            copy.start()
            sends.append(copy)
    for o in (1, 3, 2):
        remote(r_recv.at[o - 1], r_recv.at[o - 1], r_ssem.at[o - 1], r_rsem.at[o - 1], at_z(4 * o)).wait_recv()
        total = total + r_recv[o - 1].astype(F32)
    for j in range(PIECES):
        out_ref[:, j * PIECE : (j + 1) * PIECE] = total[j : j + 1].astype(BF16)
    for copy in sends:
        copy.wait_send()


def per_device(queries, latent_cache, lengths, moe_rows, expert_ids, route_gates, w_gate, w_up, w_down):
    any_spec = pl.BlockSpec(memory_space=pl.ANY)
    vmem_spec = pl.BlockSpec(memory_space=pltpu.VMEM)
    dma = pltpu.SemaphoreType.DMA
    context, out = pl.pallas_call(
        kernel,
        out_shape=(
            jax.ShapeDtypeStruct((HEADS, LATENT), BF16),
            jax.ShapeDtypeStruct((1, D), BF16),
        ),
        in_specs=[pl.BlockSpec(memory_space=pltpu.SMEM)] + [vmem_spec] * 3 + [any_spec] * 5,
        out_specs=(vmem_spec, vmem_spec),
        scratch_shapes=[
            pltpu.VMEM((WIDTH, HEADS), BF16),
            pltpu.VMEM((CTX, WIDTH), BF16),
            pltpu.VMEM((CTX, HEADS), F32),
            pltpu.VMEM((CTX, HEADS), BF16),
            pltpu.VMEM((4, HID, HALF_D), BF16),
            pltpu.VMEM((2, HID, HALF_D), BF16),
            pltpu.VMEM((2, 4, 4, 16, LANES), BF16),
            pltpu.VMEM((128, 256), F32),
            pltpu.VMEM((2, PEERS, 16, LANES), BF16),
            pltpu.VMEM((2, PEERS, 16, LANES), BF16),
            pltpu.VMEM((NY, 2, HALF, ROWS, LANES), BF16),
            pltpu.VMEM((4 * HID, 128), F32),
            pltpu.VMEM((4 * HID, 128), F32),
            pltpu.VMEM((ROWS, 4 * HID), F32),
            pltpu.VMEM((ROWS, 4 * HID), F32),
            pltpu.VMEM((NY - 1, HALF, ROWS, PIECE), F32),
            pltpu.VMEM((2, 4, HALF, ROWS, PIECE), BF16),
            pltpu.VMEM((2, 4, HALF, ROWS, PIECE), BF16),
            pltpu.VMEM((PEERS, 16, PIECE), BF16),
            pltpu.VMEM((PEERS, 16, PIECE), BF16),
            pltpu.VMEM((4, 4, 16, PIECE), BF16),
            pltpu.VMEM((3, 4, 16, PIECE), BF16),
            pltpu.VMEM((3, 16, PIECE), BF16),
            pltpu.VMEM((3, 16, PIECE), BF16),
            dma((5,)), dma((3,)), dma((3,)),
            dma((2, 3)), dma((2, 3)), dma((2, 3, 4)), dma((2, 3, 4)),
            dma((2, 7)), dma((2, 7)),
            dma((2, 4, 2, 2)), dma((2, 4, 2, 2)),
            dma((2,)), dma((2,)),
            dma((2, 4, 7)), dma((2, 4, 7)),
            dma((7,)), dma((7,)),
            dma((3, 4)), dma((3, 4)), dma((3,)), dma((3,)),
        ],
        compiler_params=pltpu.CompilerParams(
            collective_id=0, has_side_effects=True, vmem_limit_bytes=55000 * 1024
        ),
        cost_estimate=pl.CostEstimate(flops=1_000_000_000, bytes_accessed=4_000_000, transcendentals=50_000),
    )(lengths, moe_rows, expert_ids, route_gates, jnp.swapaxes(queries, 1, 2), latent_cache, w_gate, w_up, w_down)
    return context[None], out


def solution(mesh):
    rows = P(("node", "local"), None)
    wide = P(("node", "local"), None, None)
    return jax.shard_map(
        per_device,
        mesh=mesh,
        in_specs=(wide, wide, P(("node", "local")), rows, rows, rows, wide, wide, wide),
        out_specs=(wide, rows),
        check_vma=False,
    )
```
